256 devices in a mesh: row: 32 (over y, x, z_hi), col: 8 (over z_lo, core).
Axes of the slice: x: 4, y: 4, z: 8 (z_hi: 2, z_lo: 4; z = z_hi * 4 + z_lo), core: 2. Of those that a mesh axis runs over, the one named last changes fastest.
Arguments:
- factor: bfloat16 [22016, 22016], P('row', 'col'), may hold values from -3 to 3
- inverse_root: bfloat16 [22016, 22016], P('row', 'col'), may hold values from -0.078125 to 0.078125
- gradients: bfloat16 [22016, 512], P(('col', 'row')), may hold values from -1.5 to 1.5
Outputs:
- new_factor: bfloat16 [22016, 22016], P('row', 'col')
- preconditioned: bfloat16 [22016, 512], P(('row', 'col'))
The draws below stay inside these ranges and needn't reach their ends.
All inputs are finite; a program needn't handle non-finite values.
Results may differ from the reference program's by a relative error of at most 0.00175.
Values may be sent and summed in bfloat16 or wider, within the bound.
A program may use at most 64 MiB of HBM per device.

```python
import jax
import jax.numpy as jnp
from jax import lax

DIM = 22016
WIDTH = 512
N_ROW = 32


def raised(entries, rng, source, target, shards_of, factor):
    def block_of(dim):
        return (jnp.arange(entries.shape[dim]) // (entries.shape[dim] // shards_of)).reshape((-1,) + (1,) * (entries.ndim - 1 - dim))

    near = jax.random.permutation(rng, shards_of)[block_of(target)]
    other_side = (block_of(target) + shards_of // 2) % shards_of
    return jnp.where((block_of(source) == near) | (block_of(source) == other_side), factor * entries, entries)


def block_levels(rng, shape, shards, least, high):
    factor_of = 1.0
    for dim, parts in shards:
        steps = jax.random.uniform(jax.random.fold_in(jax.random.fold_in(rng, 6), dim), (parts,), jnp.float32, least / len(shards), high / len(shards))
        factor_of = factor_of * jnp.repeat(jnp.exp(steps), shape[dim] // parts).reshape((-1,) + (1,) * (len(shape) - 1 - dim))
    return factor_of


def normal_values(own_key, dims, scale, reach, split=(), kind=jnp.bfloat16):
    drawn = jax.random.normal(own_key, dims, jnp.float32) * scale
    if len(split) > 0:
        drawn = block_levels(own_key, dims, split, -0.22, 0.18) * drawn
    return jnp.clip(drawn, min=-reach, max=reach).astype(kind)


def bell_draw_with(rng, extent, deviation, reach, split, heavy, kind=jnp.bfloat16):
    array = deviation * jax.random.normal(rng, extent, jnp.float32)
    if split:
        array = array * block_levels(rng, extent, split, -0.22, 0.18)
    return jnp.clip(raised(array, jax.random.fold_in(rng, 3), *heavy), -reach, reach).astype(kind)


def setup_inputs(seed: int = 0) -> dict:
    keys = jax.random.split(jax.random.key(seed), 4)
    return {
        "factor": normal_values(keys[0], (DIM, DIM), 0.5, 3.0, ((0, 32), (1, 8))),
        "inverse_root": bell_draw_with(keys[1], (DIM, DIM), DIM ** -0.5, 0.078125, ((0, 32), (1, 8)), (1, 0, 32, 2.75)),
        "gradients": normal_values(keys[2], (DIM, WIDTH), 0.25, 1.5, ((0, 256),)),
    }


decay_rate = 0.95


def reference(factor, inverse_root, gradients):
    row_block = DIM // N_ROW
    grad_whole = gradients.astype(jnp.float32)

    def one_block(inputs):
        factor_rows, root_rows, grad_rows = inputs
        update = jnp.dot(grad_rows, grad_whole.T, precision=lax.Precision.HIGHEST)
        fresh = (decay_rate * factor_rows.astype(jnp.float32) + (1.0 - decay_rate) * update).astype(jnp.bfloat16)
        output_rows = jnp.dot(root_rows.astype(jnp.float32), grad_whole, precision=lax.Precision.HIGHEST)
        return fresh, output_rows.astype(jnp.bfloat16)

    fresh, output_rows = lax.map(one_block, (
        factor.reshape(N_ROW, row_block, DIM),
        inverse_root.reshape(N_ROW, row_block, DIM),
        grad_whole.reshape(N_ROW, row_block, grad_whole.shape[1])))
    return fresh.reshape(DIM, DIM), output_rows.reshape(DIM, grad_whole.shape[1])
```

```python
import functools

import jax
import jax.numpy as jnp
from jax import lax
from jax.experimental import pallas as pl
from jax.experimental.pallas import tpu as pltpu
from jax.sharding import PartitionSpec as P

MESH = pl.DeviceIdType.MESH
PHASES = 2
decay_rate = 0.95


def place():
    row, col = lax.axis_index("row"), lax.axis_index("col")
    return row // 8, lax.rem(row // 2, 4), lax.rem(row, 2), col // 2, lax.rem(col, 2)


def device(y, x, zh, zl, core):
    return ((y * 4 + x) * 2 + zh, zl * 2 + core)


def tiles(size, step):
    return [(start, min(step, size - start)) for start in range(0, size, step)]


def kernel(
    factor_hbm, root_hbm, grad_ref, fresh_hbm, pre_ref,
    slots, cols, own, root, factor, fresh, part, pieces, core_in, sums, line_in,
    load_sem, store_sem, twin_sem, ring_send, ring_recv, own_send, own_recv, core_sem, line_send, line_recv,
):
    y, x, zh, zl, core = place()
    rows, depth = root.shape
    share = grad_ref.shape[0]
    wide = slots.shape[-1]
    span = 2 * wide
    block = 8 * share

    load_root = pltpu.make_async_copy(root_hbm, root, load_sem.at[0])
    load_factor = pltpu.make_async_copy(factor_hbm, factor, load_sem.at[1])
    load_root.start()
    load_factor.start()

    def turned(a, k):
        return lax.rem(a + k, 4)

    barrier = pltpu.get_barrier_semaphore()
    peers = [device(y, x, 1 - zh, zl, core), device(y, x, zh, zl, 1 - core)]
    for k in (1, 2, 3):
        peers += [
            device(y, turned(x, k), zh, zl, core),
            device(turned(y, k), x, zh, zl, core),
            device(y, x, zh, turned(zl, k), core),
        ]
    for peer in peers:
        pl.semaphore_signal(barrier, inc=1, device_id=peer, device_id_type=MESH)
    for p in range(PHASES):
        for g in range(2):
            start = p * span + g * wide
            slots[g, p, zh, y, x] = grad_ref[:, start : start + wide]
    pl.semaphore_wait(barrier, len(peers))

    def twin(p, side):
        at = slots.at[:, p, side, y, x]
        return pltpu.make_async_remote_copy(
            src_ref=at, dst_ref=at, send_sem=twin_sem.at[0, p], recv_sem=twin_sem.at[1, p],
            device_id=device(y, x, 1 - zh, zl, core), device_id_type=MESH,
        )

    def ring(stage, own_side, p, g, k, arriving):
        side = zh if own_side else 1 - zh
        back = 4 - k if arriving else 0
        if (stage == 0) == (g == 0):
            across = turned(x, back)
            at = slots.at[g, p, side, y, across] if stage == 0 else slots.at[g, p, side, :, across]
            target = device(y, turned(x, k), zh, zl, core)
        else:
            across = turned(y, back)
            at = slots.at[g, p, side, across, x] if stage == 0 else slots.at[g, p, side, across]
            target = device(turned(y, k), x, zh, zl, core)
        s = (((stage * 2 + own_side) * PHASES + p) * 2 + g) * 3 + k - 1
        return pltpu.make_async_remote_copy(
            src_ref=at, dst_ref=at, send_sem=ring_send.at[s], recv_sem=ring_recv.at[s],
            device_id=target, device_id_type=MESH,
        )

    def ring_start(stage, own_side, p):
        for k in (1, 3, 2):
            for g in range(2):
                ring(stage, own_side, p, g, k, False).start()

    def ring_wait(stage, own_side, p):
        for k in (1, 3, 2):
            for g in range(2):
                ring(stage, own_side, p, g, k, True).wait_recv()

    for p in range(PHASES):
        twin(p, zh).start()
        ring_start(0, 1, p)
    for p in range(PHASES):
        ring_wait(0, 1, p)
        ring_start(1, 1, p)
    for p in range(PHASES):
        twin(p, 1 - zh).wait_recv()
        ring_start(0, 0, p)
    for p in range(PHASES):
        ring_wait(0, 0, p)
        ring_start(1, 0, p)

    own_block = lax.rem(x, 2) * 2 + zh
    source_core = x // 2

    def own_copy(p, way, from_root):
        lanes = pl.ds(p * span, span)
        here = own.at[:, lanes]
        src = cols.at[pl.ds(pl.multiple_of(own_block * block, 16), block), lanes] if from_root else here
        if way == 0:
            target = device(y, x, zh, zl, 1 - core)
        elif way == 1:
            target = device(y, x, zh, lax.rem(zl + 1, 4), core)
        else:
            target = device(y, x, zh, lax.rem(zl + 3, 4), core)
        return pltpu.make_async_remote_copy(
            src_ref=src, dst_ref=here, send_sem=own_send.at[p, way], recv_sem=own_recv.at[p],
            device_id=target, device_id_type=MESH,
        )

    is_source = core == source_core
    is_root = jnp.logical_and(is_source, zl == y)
    upward = jnp.logical_and(is_source, jnp.logical_and(zl >= y, zl < 3))
    downward = jnp.logical_and(is_source, jnp.logical_and(zl <= y, zl > 0))

    def own_start(p, from_root):
        chosen = is_root if from_root else jnp.logical_and(is_source, zl != y)

        @pl.when(jnp.logical_and(chosen, upward))
        def _():
            own_copy(p, 1, from_root).start()

        @pl.when(jnp.logical_and(chosen, downward))
        def _():
            own_copy(p, 2, from_root).start()

        @pl.when(chosen)
        def _():
            own_copy(p, 0, from_root).start()

    def own_wait_recv(p):
        @pl.when(jnp.logical_not(is_root))
        def _():
            own_copy(p, 0, False).wait_recv()

    def own_wait_send(p):
        @pl.when(upward)
        def _():
            own_copy(p, 1, False).wait_send()

        @pl.when(downward)
        def _():
            own_copy(p, 2, False).wait_send()

        @pl.when(is_source)
        def _():
            own_copy(p, 0, False).wait_send()

    def assemble(p):
        for g in range(2):
            lanes = pl.ds(p * span + g * wide, wide)

            @pl.loop(0, 4)
            def _(yy):
                parts = [slots[g, p, s % 2, yy, s // 2] for s in range(8)]
                cols[pl.ds(pl.multiple_of(yy * block, 16), block), lanes] = jnp.concatenate(parts, 0)

    def multiply(p):
        lanes = pl.ds(p * span, span)

        def some(at, size):
            part[pl.ds(at, size), :] = jnp.dot(
                root[pl.ds(at, size), :], cols[:, lanes], preferred_element_type=jnp.float32
            )

        whole = rows // 128

        @pl.loop(0, whole)
        def _(i):
            some(pl.multiple_of(i * 128, 128), 128)

        some(whole * 128, rows - whole * 128)
        for s in range(8):
            pieces[p, s % 2, s // 2] = part[s * share : (s + 1) * share, :]

    def core_copy(p):
        return pltpu.make_async_remote_copy(
            src_ref=pieces.at[p, 1 - core], dst_ref=core_in.at[p],
            send_sem=core_sem.at[0, p], recv_sem=core_sem.at[1, p],
            device_id=device(y, x, zh, zl, 1 - core), device_id_type=MESH,
        )

    def line_copy(p, k):
        return pltpu.make_async_remote_copy(
            src_ref=sums.at[p, turned(zl, k)], dst_ref=line_in.at[p, k - 1],
            send_sem=line_send.at[p, k - 1], recv_sem=line_recv.at[p, k - 1],
            device_id=device(y, x, zh, turned(zl, k), core), device_id_type=MESH,
        )

    def reduce_start(p):
        core_copy(p).wait_recv()
        for s in range(4):
            sums[p, s] = pieces[p, core, s] + core_in[p, s]
        for k in (1, 2, 3):
            line_copy(p, k).start()

    def reduce_end(p):
        for k in (1, 2, 3):
            line_copy(p, k).wait_recv()
        total = sums[p, zl] + line_in[p, 0] + line_in[p, 1] + line_in[p, 2]
        pre_ref[:, p * span : (p + 1) * span] = total.astype(pre_ref.dtype)

    load_root.wait()
    for p in range(PHASES):
        ring_wait(1, 1, p)
        ring_wait(1, 0, p)
        assemble(p)
        own_start(p, True)
        multiply(p)
        core_copy(p).start()
        own_wait_recv(p)
        own_start(p, False)
        reduce_start(p)

    @pl.when(is_root)
    def _():
        own[...] = cols[pl.ds(pl.multiple_of(own_block * block, 16), block), :]

    load_factor.wait()

    def update(at, size):
        lanes = pl.ds(at, size)
        statistic = lax.dot_general(
            own[...], cols[lanes, :], (((1,), (1,)), ((), ())), preferred_element_type=jnp.float32
        )
        mixed = decay_rate * factor[:, lanes].astype(jnp.float32) + (1.0 - decay_rate) * statistic
        fresh[:, lanes] = mixed.astype(fresh.dtype)

    steps = tiles(depth, 256)

    @pl.loop(0, depth // 256)
    def _(i):
        update(pl.multiple_of(i * 256, 256), 256)

    if depth % 256:
        update(*steps[-1])
    store = pltpu.make_async_copy(fresh, fresh_hbm, store_sem.at[0])
    store.start()
    for p in range(PHASES):
        reduce_end(p)
    for p in range(PHASES):
        twin(p, zh).wait_send()
        for stage in range(2):
            for own_side in range(2):
                for k in (1, 2, 3):
                    for g in range(2):
                        ring(stage, own_side, p, g, k, False).wait_send()
        own_wait_send(p)
        core_copy(p).wait_send()
        for k in (1, 2, 3):
            line_copy(p, k).wait_send()
    store.wait()


def per_device(factor, inverse_root, gradients):
    rows, depth = factor.shape
    share, width = gradients.shape
    wide = width // (2 * PHASES)
    span = 2 * wide
    bf16, f32 = jnp.bfloat16, jnp.float32
    dma = pltpu.SemaphoreType.DMA
    flops = 4 * rows * depth * width
    return pl.pallas_call(
        kernel,
        out_shape=(
            jax.ShapeDtypeStruct(factor.shape, bf16),
            jax.ShapeDtypeStruct((share, width), bf16),
        ),
        in_specs=[
            pl.BlockSpec(memory_space=pl.ANY),
            pl.BlockSpec(memory_space=pl.ANY),
            pl.BlockSpec(memory_space=pltpu.VMEM),
        ],
        out_specs=(pl.BlockSpec(memory_space=pl.ANY), pl.BlockSpec(memory_space=pltpu.VMEM)),
        scratch_shapes=[
            pltpu.VMEM((2, PHASES, 2, 4, 4, share, wide), bf16),
            pltpu.VMEM((depth, width), bf16),
            pltpu.VMEM((rows, width), bf16),
            pltpu.VMEM((rows, depth), bf16),
            pltpu.VMEM((rows, depth), bf16),
            pltpu.VMEM((rows, depth), bf16),
            pltpu.VMEM((rows, span), f32),
            pltpu.VMEM((PHASES, 2, 4, share, span), f32),
            pltpu.VMEM((PHASES, 4, share, span), f32),
            pltpu.VMEM((PHASES, 4, share, span), f32),
            pltpu.VMEM((PHASES, 3, share, span), f32),
            dma((2,)),
            dma((1,)),
            dma((2, PHASES)),
            dma((24 * PHASES,)),
            dma((24 * PHASES,)),
            dma((PHASES, 3)),
            dma((PHASES,)),
            dma((2, PHASES)),
            dma((PHASES, 3)),
            dma((PHASES, 3)),
        ],
        compiler_params=pltpu.CompilerParams(
            collective_id=0, has_side_effects=True, vmem_limit_bytes=56 * 1024 * 1024
        ),
        cost_estimate=pl.CostEstimate(flops=flops, bytes_accessed=6 * rows * depth, transcendentals=0),
    )(factor, inverse_root, gradients)


def solution(mesh):
    placed = (P("row", "col"), P("row", "col"), P(("col", "row"), None))
    return jax.shard_map(
        per_device,
        mesh=mesh,
        in_specs=placed,
        out_specs=(P("row", "col"), P(("row", "col"), None)),
        check_vma=False,
    )
```

```python
import functools

import jax
import jax.numpy as jnp
from jax import lax
from jax.experimental import pallas as pl
from jax.experimental.pallas import tpu as pltpu
from jax.sharding import PartitionSpec as P

MESH = pl.DeviceIdType.MESH
PHASES = 2
CHUNKS = 4
decay_rate = 0.95


def place():
    row, col = lax.axis_index("row"), lax.axis_index("col")
    return row // 8, lax.rem(row // 2, 4), lax.rem(row, 2), col // 2, lax.rem(col, 2)


def device(y, x, zh, zl, core):
    return ((y * 4 + x) * 2 + zh, zl * 2 + core)


def tiles(size, step):
    return [(start, min(step, size - start)) for start in range(0, size, step)]


def kernel(
    factor_hbm, root_hbm, grad_hbm, fresh, pre_ref,
    grad_ref, slots, cols, own, root, factor, part, pieces, core_in, sums, line_in, relay_in,
    load_sem, twin_sem, near_send, near_recv, far_send, far_recv, own_send, own_recv, core_sem, line_send, line_recv, relay_sem,
):
    y, x, zh, zl, core = place()
    rows, depth = root.shape
    share = grad_hbm.shape[0]
    wide = slots.shape[-1]
    span = 2 * wide
    block = 8 * share

    load_root = pltpu.make_async_copy(root_hbm, root, load_sem.at[0])
    load_factor = pltpu.make_async_copy(factor_hbm, factor, load_sem.at[1])
    load_grad = pltpu.make_async_copy(grad_hbm, grad_ref, load_sem.at[2])
    load_grad.start()

    def turned(a, k):
        return lax.rem(a + k, 4)

    barrier = pltpu.get_barrier_semaphore()
    peers = [device(y, x, 1 - zh, zl, core), device(y, x, zh, zl, 1 - core)]
    for k in (1, 2, 3):
        peers += [
            device(y, turned(x, k), zh, zl, core),
            device(turned(y, k), x, zh, zl, core),
            device(y, x, zh, turned(zl, k), core),
        ]
    level = zh * 4 + zl
    wrap = lax.rem(jnp.where(zl == 0, level + 7, level + 1), 8)
    outer = device(y, x, wrap // 4, lax.rem(wrap, 4), core)
    for peer in peers:
        pl.semaphore_signal(barrier, inc=1, device_id=peer, device_id_type=MESH)
    load_grad.wait()
    load_root.start()
    load_factor.start()
    for p in range(PHASES):
        for g in range(2):
            start = p * span + g * wide
            slots[g, p, zh, y, x] = grad_ref[:, start : start + wide]
    edge = jnp.logical_or(zl == 0, zl == 3)

    @pl.when(edge)
    def _():
        pl.semaphore_signal(barrier, inc=1, device_id=outer, device_id_type=MESH)

    pl.semaphore_wait(barrier, jnp.where(edge, len(peers) + 1, len(peers)))

    def twin(p, side):
        at = slots.at[:, p, side, y, x]
        return pltpu.make_async_remote_copy(
            src_ref=at, dst_ref=at, send_sem=twin_sem.at[0, p], recv_sem=twin_sem.at[1, p],
            device_id=device(y, x, 1 - zh, zl, core), device_id_type=MESH,
        )

    def near(own_side, p, g, k, arriving):
        side = zh if own_side else 1 - zh
        back = 4 - k if arriving else 0
        if g == 0:
            at = slots.at[g, p, side, y, turned(x, back)]
            target = device(y, turned(x, k), zh, zl, core)
        else:
            at = slots.at[g, p, side, turned(y, back), x]
            target = device(turned(y, k), x, zh, zl, core)
        s = ((own_side * PHASES + p) * 2 + g) * 3 + k - 1
        return pltpu.make_async_remote_copy(
            src_ref=at, dst_ref=at, send_sem=near_send.at[s], recv_sem=near_recv.at[s],
            device_id=target, device_id_type=MESH,
        )

    def far(own_side, p, g, k, half, origin):
        side = zh if own_side else 1 - zh
        part_of = pl.ds(half * 2, 2)
        if g == 0:
            at = slots.at[g, p, side, turned(y, origin), part_of]
            target = device(turned(y, k), x, zh, zl, core)
        else:
            at = slots.at[g, p, side, part_of, turned(x, origin)]
            target = device(y, turned(x, k), zh, zl, core)
        lane = (0 if k == 1 else 1) if origin == 0 else 2
        s = (((own_side * PHASES + p) * 2 + g) * 3 + lane) * 2 + half
        return pltpu.make_async_remote_copy(
            src_ref=at, dst_ref=at, send_sem=far_send.at[s], recv_sem=far_recv.at[s],
            device_id=target, device_id_type=MESH,
        )

    def far_landed(own_side, p, g, k, half, origin):
        side = zh if own_side else 1 - zh
        part_of = pl.ds(half * 2, 2)
        if g == 0:
            at = slots.at[g, p, side, turned(y, origin), part_of]
            target = device(turned(y, k), x, zh, zl, core)
        else:
            at = slots.at[g, p, side, part_of, turned(x, origin)]
            target = device(y, turned(x, k), zh, zl, core)
        lane = 2 if origin == 2 else (0 if k == 1 else 1)
        s = (((own_side * PHASES + p) * 2 + g) * 3 + lane) * 2 + half
        return pltpu.make_async_remote_copy(
            src_ref=at, dst_ref=at, send_sem=far_send.at[s], recv_sem=far_recv.at[s],
            device_id=target, device_id_type=MESH,
        )

    def near_start(own_side, p):
        for k in (1, 3, 2):
            for g in range(2):
                near(own_side, p, g, k, False).start()

    def near_wait(own_side, p):
        for k in (1, 3, 2):
            for g in range(2):
                near(own_side, p, g, k, True).wait_recv()

    def far_start(own_side, p):
        for step in range(2):
            for g in range(2):
                far(own_side, p, g, 1, step, 0).start()
                far(own_side, p, g, 3, 1 - step, 0).start()

    def far_pass(own_side, p):
        for g in range(2):
            far_landed(own_side, p, g, 1, 0, 3).wait_recv()
            far(own_side, p, g, 1, 0, 3).start()
            far_landed(own_side, p, g, 3, 1, 1).wait_recv()
            far(own_side, p, g, 3, 1, 1).start()

    def far_wait(own_side, p):
        for g in range(2):
            far_landed(own_side, p, g, 1, 1, 3).wait_recv()
            far_landed(own_side, p, g, 3, 0, 1).wait_recv()
            far_landed(own_side, p, g, 1, 0, 2).wait_recv()
            far_landed(own_side, p, g, 3, 1, 2).wait_recv()

    def gather_sent(p):
        for own_side in range(2):
            for g in range(2):
                for k in (1, 2, 3):
                    near(own_side, p, g, k, False).wait_send()
                for half in range(2):
                    far(own_side, p, g, 1, half, 0).wait_send()
                    far(own_side, p, g, 3, half, 0).wait_send()
                far(own_side, p, g, 1, 0, 3).wait_send()
                far(own_side, p, g, 3, 1, 1).wait_send()

    for p in range(PHASES):
        twin(p, zh).start()
        near_start(1, p)
    near_wait(1, 0)
    far_start(1, 0)
    near_wait(1, 1)
    twin(0, 1 - zh).wait_recv()
    near_start(0, 0)
    far_start(1, 1)
    twin(1, 1 - zh).wait_recv()
    far_pass(1, 0)
    near_wait(0, 0)
    far_start(0, 0)
    near_start(0, 1)
    far_pass(1, 1)
    near_wait(0, 1)
    far_pass(0, 0)
    far_start(0, 1)

    source_core = x // 2
    is_source = core == source_core
    apart = lax.rem(zl + 4 - y, 4)
    is_root = jnp.logical_and(is_source, apart == 0)
    passes = jnp.logical_and(is_source, jnp.logical_or(
        jnp.logical_and(apart == 1, y < 2), jnp.logical_and(apart == 3, y >= 2)))
    chunk = own.shape[0] // CHUNKS // 16 * 16
    chunks = [(c * chunk, chunk if c < CHUNKS - 1 else rows - c * chunk) for c in range(CHUNKS)]

    def line_device(step, to_core):
        level = zh * 4 + zl
        level = lax.rem(level + step, 8)
        return device(y, x, level // 4, lax.rem(level, 4), to_core)

    def own_copy(p, c, way, from_root):
        lanes = pl.ds(p * span, span)
        at, size = chunks[c]
        here = own.at[pl.ds(at, size), lanes]
        if way == 0:
            target, side = device(y, x, zh, zl, 1 - core), zh
        elif way == 3:
            target, side = line_device(jnp.where(y < 2, 1, 7), core), zh
        else:
            step = 1 if way == 1 else 7
            target = line_device(step, core)
            side = lax.rem(zh * 4 + zl + step, 8) // 4
        src = here
        if from_root:
            base = pl.multiple_of((lax.rem(x, 2) * 2 + side) * block, 16)
            src = cols.at[pl.ds(base + at, size), lanes]
        slot = (0 if way == 0 else 1 if way in (1, 3) else 2)
        return pltpu.make_async_remote_copy(
            src_ref=src, dst_ref=here, send_sem=own_send.at[p, c, slot], recv_sem=own_recv.at[p, c],
            device_id=target, device_id_type=MESH,
        )

    def own_start(p):
        @pl.when(is_root)
        def _():
            for c in range(CHUNKS):
                own_copy(p, c, 1, True).start()
                own_copy(p, c, 2, True).start()
            for c in range(CHUNKS):
                own_copy(p, c, 0, True).start()

    def own_pass(p):
        for c in range(CHUNKS):
            @pl.when(jnp.logical_not(is_root))
            def _():
                own_copy(p, c, 0, False).wait_recv()

            @pl.when(passes)
            def _():
                own_copy(p, c, 3, False).start()

            @pl.when(jnp.logical_and(is_source, apart != 0))
            def _():
                own_copy(p, c, 0, False).start()

    def own_sent(p):
        for c in range(CHUNKS):
            @pl.when(jnp.logical_or(is_root, passes))
            def _():
                own_copy(p, c, 1, False).wait_send()

            @pl.when(is_root)
            def _():
                own_copy(p, c, 2, False).wait_send()

            @pl.when(is_source)
            def _():
                own_copy(p, c, 0, False).wait_send()

    def assemble(p):
        for g in range(2):
            lanes = pl.ds(p * span + g * wide, wide)

            @pl.loop(0, 4)
            def _(yy):
                parts = [slots[g, p, s % 2, yy, s // 2] for s in range(8)]
                cols[pl.ds(pl.multiple_of(yy * block, 16), block), lanes] = jnp.concatenate(parts, 0)

    def multiply(p):
        lanes = pl.ds(p * span, span)

        def some(at, size):
            part[pl.ds(at, size), :] = jnp.dot(
                root[pl.ds(at, size), :], cols[:, lanes], preferred_element_type=jnp.float32
            )

        half = rows // 32 * 16
        some(0, half)
        some(half, rows - half)
        for s in range(8):
            pieces[p, s % 2, s // 2] = part[s * share : (s + 1) * share, :]

    def core_copy(p):
        return pltpu.make_async_remote_copy(
            src_ref=pieces.at[p, 1 - core], dst_ref=core_in.at[p],
            send_sem=core_sem.at[0, p], recv_sem=core_sem.at[1, p],
            device_id=device(y, x, zh, zl, 1 - core), device_id_type=MESH,
        )

    def line_copy(p, k):
        return pltpu.make_async_remote_copy(
            src_ref=sums.at[p, turned(zl, k)], dst_ref=line_in.at[p, k - 1],
            send_sem=line_send.at[p, k - 1], recv_sem=line_recv.at[p, k - 1],
            device_id=device(y, x, zh, turned(zl, k), core), device_id_type=MESH,
        )

    inner = jnp.logical_not(edge)
    inward = jnp.where(zl == 0, 1, 3)

    def relay_copy(p):
        return pltpu.make_async_remote_copy(
            src_ref=sums.at[p, 3 - zl], dst_ref=relay_in.at[p],
            send_sem=relay_sem.at[0, p], recv_sem=relay_sem.at[1, p],
            device_id=device(y, x, zh, turned(zl, inward), core), device_id_type=MESH,
        )

    def reduce_start(p):
        core_copy(p).wait_recv()
        for s in range(4):
            sums[p, s] = pieces[p, core, s] + core_in[p, s]

        @pl.when(edge)
        def _():
            relay_copy(p).start()
            line_copy(p, 2).start()
            line_copy(p, inward).start()

        @pl.when(inner)
        def _():
            line_copy(p, 1).start()
            line_copy(p, 3).start()

    def reduce_relay(p):
        @pl.when(inner)
        def _():
            relay_copy(p).wait_recv()
            sums[p, turned(zl, 2)] += relay_in[p]
            line_copy(p, 2).start()

    def reduce_end(p):
        line_copy(p, 2).wait_recv()

        @pl.when(zl > 0)
        def _():
            line_copy(p, 1).wait_recv()
            sums[p, zl] += line_in[p, 0]

        @pl.when(zl < 3)
        def _():
            line_copy(p, 3).wait_recv()
            sums[p, zl] += line_in[p, 2]

        total = sums[p, zl] + line_in[p, 1]
        pre_ref[:, p * span : (p + 1) * span] = total.astype(pre_ref.dtype)

    def reduce_sent(p):
        line_copy(p, 2).wait_send()

        @pl.when(edge)
        def _():
            relay_copy(p).wait_send()

        @pl.when(zl < 3)
        def _():
            line_copy(p, 1).wait_send()

        @pl.when(zl > 0)
        def _():
            line_copy(p, 3).wait_send()

    load_root.wait()
    far_wait(1, 0)
    far_wait(0, 0)
    assemble(0)
    own_start(0)
    far_pass(0, 1)
    multiply(0)
    core_copy(0).start()
    reduce_start(0)
    reduce_relay(0)
    far_wait(1, 1)
    far_wait(0, 1)
    assemble(1)
    own_start(1)
    multiply(1)
    core_copy(1).start()
    own_pass(0)
    reduce_start(1)
    reduce_relay(1)
    own_pass(1)

    @pl.when(is_root)
    def _():
        own[...] = cols[pl.ds(pl.multiple_of((lax.rem(x, 2) * 2 + zh) * block, 16), block), :]

    load_factor.wait()

    def update(at, size):
        lanes = pl.ds(at, size)
        statistic = lax.dot_general(
            own[...], cols[lanes, :], (((1,), (1,)), ((), ())), preferred_element_type=jnp.float32
        )
        mixed = decay_rate * factor[:, lanes].astype(jnp.float32) + (1.0 - decay_rate) * statistic
        fresh[:, lanes] = mixed.astype(fresh.dtype)

    steps = tiles(depth, 256)

    @pl.loop(0, depth // 256)
    def _(i):
        update(pl.multiple_of(i * 256, 256), 256)

    if depth % 256:
        update(*steps[-1])
    for p in range(PHASES):
        reduce_end(p)
    for p in range(PHASES):
        twin(p, zh).wait_send()
        gather_sent(p)
        own_sent(p)
        core_copy(p).wait_send()
        reduce_sent(p)


def per_device(factor, inverse_root, gradients):
    rows, depth = factor.shape
    share, width = gradients.shape
    wide = width // (2 * PHASES)
    span = 2 * wide
    bf16, f32 = jnp.bfloat16, jnp.float32
    dma = pltpu.SemaphoreType.DMA
    flops = 4 * rows * depth * width
    return pl.pallas_call(
        kernel,
        out_shape=(
            pltpu.VMEM(factor.shape, bf16),
            pltpu.VMEM((share, width), bf16),
        ),
        in_specs=[
            pl.BlockSpec(memory_space=pltpu.HBM),
            pl.BlockSpec(memory_space=pltpu.HBM),
            pl.BlockSpec(memory_space=pltpu.HBM),
        ],
        out_specs=(pl.BlockSpec(memory_space=pltpu.VMEM), pl.BlockSpec(memory_space=pltpu.VMEM)),
        scratch_shapes=[
            pltpu.VMEM((share, width), bf16),
            pltpu.VMEM((2, PHASES, 2, 4, 4, share, wide), bf16),
            pltpu.VMEM((depth, width), bf16),
            pltpu.VMEM((rows, width), bf16),
            pltpu.VMEM((rows, depth), bf16),
            pltpu.VMEM((rows, depth), bf16),
            pltpu.VMEM((rows, span), f32),
            pltpu.VMEM((PHASES, 2, 4, share, span), f32),
            pltpu.VMEM((PHASES, 4, share, span), f32),
            pltpu.VMEM((PHASES, 4, share, span), f32),
            pltpu.VMEM((PHASES, 3, share, span), f32),
            pltpu.VMEM((PHASES, share, span), f32),
            dma((3,)),
            dma((2, PHASES)),
            dma((12 * PHASES,)),
            dma((12 * PHASES,)),
            dma((24 * PHASES,)),
            dma((24 * PHASES,)),
            dma((PHASES, CHUNKS, 3)),
            dma((PHASES, CHUNKS)),
            dma((2, PHASES)),
            dma((PHASES, 3)),
            dma((PHASES, 3)),
            dma((2, PHASES)),
        ],
        compiler_params=pltpu.CompilerParams(
            collective_id=0, has_side_effects=True, vmem_limit_bytes=48 * 1024 * 1024
        ),
        cost_estimate=pl.CostEstimate(flops=flops, bytes_accessed=6 * rows * depth, transcendentals=0),
    )(factor, inverse_root, gradients)


def solution(mesh):
    placed = (P("row", "col"), P("row", "col"), P(("col", "row"), None))
    return jax.shard_map(
        per_device,
        mesh=mesh,
        in_specs=placed,
        out_specs=(P("row", "col"), P(("row", "col"), None)),
        check_vma=False,
    )
```

```python
import functools

import jax
import jax.numpy as jnp
from jax import lax
from jax.experimental import pallas as pl
from jax.experimental.pallas import tpu as pltpu
from jax.sharding import PartitionSpec as P

MESH = pl.DeviceIdType.MESH
PHASES = 4
decay_rate = 0.95


def place():
    row, col = lax.axis_index("row"), lax.axis_index("col")
    return row // 8, lax.rem(row // 2, 4), lax.rem(row, 2), col // 2, lax.rem(col, 2)


def device(y, x, zh, zl, core):
    return ((y * 4 + x) * 2 + zh, zl * 2 + core)


def tiles(size, step):
    return [(start, min(step, size - start)) for start in range(0, size, step)]


def kernel(
    factor_hbm, root_hbm, grad_hbm, fresh, pre_ref,
    grad_ref, slots, own_in, cols, own, root, factor, part, pieces, core_in, sums, line_in, relay_in,
    load_sem, twin_sem, near_send, near_recv, far_send, far_recv, own_send, own_recv, across_sem, core_sem, line_send, line_recv, relay_sem,
):
    y, x, zh, zl, core = place()
    rows, depth = root.shape
    share = grad_hbm.shape[0]
    span = slots.shape[-1]
    block = 8 * share

    load_root = pltpu.make_async_copy(root_hbm, root, load_sem.at[0])
    load_factor = pltpu.make_async_copy(factor_hbm, factor, load_sem.at[1])
    load_grad = pltpu.make_async_copy(grad_hbm, grad_ref, load_sem.at[2])
    load_grad.start()

    def turned(a, k):
        return lax.rem(a + k, 4)

    barrier = pltpu.get_barrier_semaphore()
    peers = [device(y, x, 1 - zh, zl, core), device(y, x, zh, zl, 1 - core)]
    for k in (1, 2, 3):
        peers += [device(y, turned(x, k), zh, zl, core), device(turned(y, k), x, zh, zl, core)]
    for step in (1, 2, 3, 5, 6, 7):
        level = lax.rem(zh * 4 + zl + step, 8)
        peers.append(device(y, x, level // 4, lax.rem(level, 4), core))
    for peer in peers:
        pl.semaphore_signal(barrier, inc=1, device_id=peer, device_id_type=MESH)
    load_grad.wait()
    load_root.start()
    load_factor.start()
    for p in range(PHASES):
        slots[p, zh, y, x] = grad_ref[:, p * span : (p + 1) * span]
    pl.semaphore_wait(barrier, len(peers))
    edge = jnp.logical_or(zl == 0, zl == 3)

    def twin(p, side):
        at = slots.at[p, side, y, x]
        return pltpu.make_async_remote_copy(
            src_ref=at, dst_ref=at, send_sem=twin_sem.at[0, p], recv_sem=twin_sem.at[1, p],
            device_id=device(y, x, 1 - zh, zl, core), device_id_type=MESH,
        )

    def x_first(own_side, p):
        return (own_side + p) % 2 == 1

    def near(own_side, p, k, arriving):
        side = zh if own_side else 1 - zh
        back = 4 - k if arriving else 0
        if x_first(own_side, p):
            at = slots.at[p, side, y, turned(x, back)]
            target = device(y, turned(x, k), zh, zl, core)
        else:
            at = slots.at[p, side, turned(y, back), x]
            target = device(turned(y, k), x, zh, zl, core)
        s = (own_side * PHASES + p) * 3 + k - 1
        return pltpu.make_async_remote_copy(
            src_ref=at, dst_ref=at, send_sem=near_send.at[s], recv_sem=near_recv.at[s],
            device_id=target, device_id_type=MESH,
        )

    def far(own_side, p, k, half, origin, lane):
        side = zh if own_side else 1 - zh
        part_of = pl.ds(half * 2, 2)
        if x_first(own_side, p):
            at = slots.at[p, side, turned(y, origin), part_of]
            target = device(turned(y, k), x, zh, zl, core)
        else:
            at = slots.at[p, side, part_of, turned(x, origin)]
            target = device(y, turned(x, k), zh, zl, core)
        s = ((own_side * PHASES + p) * 3 + lane) * 2 + half
        return pltpu.make_async_remote_copy(
            src_ref=at, dst_ref=at, send_sem=far_send.at[s], recv_sem=far_recv.at[s],
            device_id=target, device_id_type=MESH,
        )

    def near_start(own_side, p):
        for k in (2, 1, 3):
            near(own_side, p, k, False).start()

    def far_start(own_side, p):
        for k in (1, 3, 2):
            near(own_side, p, k, True).wait_recv()
        for step in range(2):
            far(own_side, p, 1, step, 0, 0).start()
            far(own_side, p, 3, 1 - step, 0, 1).start()

    def far_pass(own_side, p):
        far(own_side, p, 1, 0, 3, 0).wait_recv()
        far(own_side, p, 1, 0, 3, 2).start()
        far(own_side, p, 3, 1, 1, 1).wait_recv()
        far(own_side, p, 3, 1, 1, 2).start()

    def far_wait(own_side, p):
        far(own_side, p, 1, 1, 3, 0).wait_recv()
        far(own_side, p, 3, 0, 1, 1).wait_recv()
        far(own_side, p, 1, 0, 2, 2).wait_recv()
        far(own_side, p, 3, 1, 2, 2).wait_recv()

    def gather_sent(p):
        for own_side in range(2):
            for k in (1, 2, 3):
                near(own_side, p, k, False).wait_send()
            for half in range(2):
                far(own_side, p, 1, half, 0, 0).wait_send()
                far(own_side, p, 3, half, 0, 1).wait_send()
            far(own_side, p, 1, 0, 3, 2).wait_send()
            far(own_side, p, 3, 1, 1, 2).wait_send()

    def twin_near(p):
        twin(p, 1 - zh).wait_recv()
        near_start(0, p)

    is_source = core == x // 2
    at_root = zl == y
    is_root = jnp.logical_and(is_source, at_root)
    is_end = jnp.logical_and(is_source, jnp.logical_not(at_root))

    def own_block(side):
        return lax.rem(x, 2) * 2 + side

    def own_far(p, n):
        step = (1, 7, 2, 6, 3, 5)[n]
        level = lax.rem(zh * 4 + zl + step, 8)
        return pltpu.make_async_remote_copy(
            src_ref=slots.at[p, zh, own_block(level // 4)], dst_ref=own_in.at[p, zh],
            send_sem=own_send.at[p, n], recv_sem=own_recv.at[p, zh],
            device_id=device(y, x, level // 4, lax.rem(level, 4), core), device_id_type=MESH,
        )

    def own_landed(p, side):
        at = own_in.at[p, side]
        return pltpu.make_async_remote_copy(
            src_ref=at, dst_ref=at, send_sem=own_send.at[p, 0], recv_sem=own_recv.at[p, side],
            device_id=device(y, x, zh, zl, 1 - core), device_id_type=MESH,
        )

    def own_across(p, from_root):
        lanes = pl.ds(p * span, span)
        here = own.at[:, lanes]
        src = here
        if from_root:
            src = cols.at[pl.ds(pl.multiple_of(own_block(zh) * block, 16), block), lanes]
        return pltpu.make_async_remote_copy(
            src_ref=src, dst_ref=here, send_sem=across_sem.at[0, p], recv_sem=across_sem.at[1, p],
            device_id=device(y, x, zh, zl, 1 - core), device_id_type=MESH,
        )

    def own_start(p):
        far_wait(1, p)

        @pl.when(is_root)
        def _():
            for n in range(6):
                own_far(p, n).start()

    def own_pass(p):
        @pl.when(is_root)
        def _():
            own_across(p, True).start()

        @pl.when(is_end)
        def _():
            own_landed(p, 0).wait_recv()
            own_landed(p, 1).wait_recv()
            parts = [own_in[p, s % 2, s // 2] for s in range(8)]
            own[:, pl.ds(p * span, span)] = jnp.concatenate(parts, 0)
            own_across(p, False).start()

    def own_wait(p):
        @pl.when(jnp.logical_not(is_source))
        def _():
            own_across(p, False).wait_recv()

    def own_sent(p):
        @pl.when(is_root)
        def _():
            for n in range(6):
                own_far(p, n).wait_send()

        @pl.when(is_source)
        def _():
            own_across(p, False).wait_send()

    def assemble(p):
        lanes = pl.ds(p * span, span)

        @pl.loop(0, 4)
        def _(yy):
            parts = [slots[p, s % 2, yy, s // 2] for s in range(8)]
            cols[pl.ds(pl.multiple_of(yy * block, 16), block), lanes] = jnp.concatenate(parts, 0)

    def multiply(p):
        lanes = pl.ds(p * span, span)

        def some(at, size):
            part[pl.ds(at, size), :] = jnp.dot(
                root[pl.ds(at, size), :], cols[:, lanes], preferred_element_type=jnp.float32
            )

        half = rows // 32 * 16
        some(0, half)
        some(half, rows - half)
        for s in range(8):
            pieces[p, s % 2, s // 2] = part[s * share : (s + 1) * share, :]

    def core_copy(p):
        return pltpu.make_async_remote_copy(
            src_ref=pieces.at[p, 1 - core], dst_ref=core_in.at[p],
            send_sem=core_sem.at[0, p], recv_sem=core_sem.at[1, p],
            device_id=device(y, x, zh, zl, 1 - core), device_id_type=MESH,
        )

    def line_copy(p, k):
        return pltpu.make_async_remote_copy(
            src_ref=sums.at[p, turned(zl, k)], dst_ref=line_in.at[p, k - 1],
            send_sem=line_send.at[p, k - 1], recv_sem=line_recv.at[p, k - 1],
            device_id=device(y, x, zh, turned(zl, k), core), device_id_type=MESH,
        )

    inner = jnp.logical_not(edge)
    inward = jnp.where(zl == 0, 1, 3)

    def relay_copy(p):
        return pltpu.make_async_remote_copy(
            src_ref=sums.at[p, 3 - zl], dst_ref=relay_in.at[p],
            send_sem=relay_sem.at[0, p], recv_sem=relay_sem.at[1, p],
            device_id=device(y, x, zh, turned(zl, inward), core), device_id_type=MESH,
        )

    def reduce_start(p):
        core_copy(p).wait_recv()
        for s in range(4):
            sums[p, s] = pieces[p, core, s] + core_in[p, s]

        @pl.when(edge)
        def _():
            relay_copy(p).start()
            line_copy(p, 2).start()
            line_copy(p, inward).start()

        @pl.when(inner)
        def _():
            line_copy(p, 1).start()
            line_copy(p, 3).start()

    def reduce_relay(p):
        @pl.when(inner)
        def _():
            relay_copy(p).wait_recv()
            sums[p, turned(zl, 2)] += relay_in[p]
            line_copy(p, 2).start()

    def reduce_end(p):
        line_copy(p, 2).wait_recv()

        @pl.when(zl > 0)
        def _():
            line_copy(p, 1).wait_recv()
            sums[p, zl] += line_in[p, 0]

        @pl.when(zl < 3)
        def _():
            line_copy(p, 3).wait_recv()
            sums[p, zl] += line_in[p, 2]

        total = sums[p, zl] + line_in[p, 1]
        pre_ref[:, p * span : (p + 1) * span] = total.astype(pre_ref.dtype)

    def reduce_sent(p):
        line_copy(p, 2).wait_send()

        @pl.when(edge)
        def _():
            relay_copy(p).wait_send()

        @pl.when(zl < 3)
        def _():
            line_copy(p, 1).wait_send()

        @pl.when(zl > 0)
        def _():
            line_copy(p, 3).wait_send()

    def finish(p):
        far_wait(0, p)
        assemble(p)
        multiply(p)
        core_copy(p).start()

    twin(0, zh).start()
    near_start(1, 0)
    twin(1, zh).start()
    near_start(1, 1)
    twin(2, zh).start()
    near_start(1, 2)
    twin(3, zh).start()
    near_start(1, 3)
    far_start(1, 0)
    far_start(1, 1)
    far_start(1, 2)
    far_start(1, 3)
    twin_near(0)
    twin_near(1)
    twin_near(2)
    twin_near(3)
    far_pass(1, 0)
    far_pass(1, 1)
    far_start(0, 0)
    own_start(0)
    far_pass(1, 2)
    far_start(0, 1)
    own_start(1)
    far_pass(1, 3)
    far_start(0, 2)
    own_start(2)
    far_pass(0, 0)
    far_start(0, 3)
    own_start(3)
    far_pass(0, 1)
    far_pass(0, 2)

    load_root.wait()
    finish(0)
    far_pass(0, 3)
    reduce_start(0)
    own_pass(0)
    finish(1)
    reduce_start(1)
    reduce_relay(0)
    finish(2)
    reduce_start(2)
    own_pass(1)
    reduce_relay(1)
    finish(3)
    reduce_start(3)
    own_pass(2)
    own_pass(3)
    reduce_relay(2)
    reduce_relay(3)

    for p in range(PHASES):
        own_wait(p)

    @pl.when(is_root)
    def _():
        own[...] = cols[pl.ds(pl.multiple_of(own_block(zh) * block, 16), block), :]

    load_factor.wait()

    def update(at, size):
        lanes = pl.ds(at, size)
        statistic = lax.dot_general(
            own[...], cols[lanes, :], (((1,), (1,)), ((), ())), preferred_element_type=jnp.float32
        )
        mixed = decay_rate * factor[:, lanes].astype(jnp.float32) + (1.0 - decay_rate) * statistic
        fresh[:, lanes] = mixed.astype(fresh.dtype)

    steps = tiles(depth, 256)

    @pl.loop(0, depth // 256)
    def _(i):
        update(pl.multiple_of(i * 256, 256), 256)

    if depth % 256:
        update(*steps[-1])
    for p in range(PHASES):
        reduce_end(p)
    for p in range(PHASES):
        twin(p, zh).wait_send()
        gather_sent(p)
        own_sent(p)
        core_copy(p).wait_send()
        reduce_sent(p)


def per_device(factor, inverse_root, gradients):
    rows, depth = factor.shape
    share, width = gradients.shape
    span = width // PHASES
    bf16, f32 = jnp.bfloat16, jnp.float32
    dma = pltpu.SemaphoreType.DMA
    flops = 4 * rows * depth * width
    return pl.pallas_call(
        kernel,
        out_shape=(
            pltpu.VMEM(factor.shape, bf16),
            pltpu.VMEM((share, width), bf16),
        ),
        in_specs=[
            pl.BlockSpec(memory_space=pltpu.HBM),
            pl.BlockSpec(memory_space=pltpu.HBM),
            pl.BlockSpec(memory_space=pltpu.HBM),
        ],
        out_specs=(pl.BlockSpec(memory_space=pltpu.VMEM), pl.BlockSpec(memory_space=pltpu.VMEM)),
        scratch_shapes=[
            pltpu.VMEM((share, width), bf16),
            pltpu.VMEM((PHASES, 2, 4, 4, share, span), bf16),
            pltpu.VMEM((PHASES, 2, 4, share, span), bf16),
            pltpu.VMEM((depth, width), bf16),
            pltpu.VMEM((rows, width), bf16),
            pltpu.VMEM((rows, depth), bf16),
            pltpu.VMEM((rows, depth), bf16),
            pltpu.VMEM((rows, span), f32),
            pltpu.VMEM((PHASES, 2, 4, share, span), f32),
            pltpu.VMEM((PHASES, 4, share, span), f32),
            pltpu.VMEM((PHASES, 4, share, span), f32),
            pltpu.VMEM((PHASES, 3, share, span), f32),
            pltpu.VMEM((PHASES, share, span), f32),
            dma((3,)),
            dma((2, PHASES)),
            dma((6 * PHASES,)),
            dma((6 * PHASES,)),
            dma((12 * PHASES,)),
            dma((12 * PHASES,)),
            dma((PHASES, 6)),
            dma((PHASES, 2)),
            dma((2, PHASES)),
            dma((2, PHASES)),
            dma((PHASES, 3)),
            dma((PHASES, 3)),
            dma((2, PHASES)),
        ],
        compiler_params=pltpu.CompilerParams(
            collective_id=0, has_side_effects=True, vmem_limit_bytes=48 * 1024 * 1024
        ),
        cost_estimate=pl.CostEstimate(flops=flops, bytes_accessed=6 * rows * depth, transcendentals=0),
    )(factor, inverse_root, gradients)


def solution(mesh):
    placed = (P("row", "col"), P("row", "col"), P(("col", "row"), None))
    return jax.shard_map(
        per_device,
        mesh=mesh,
        in_specs=placed,
        out_specs=(P("row", "col"), P(("row", "col"), None)),
        check_vma=False,
    )
```

```python
import functools

import jax
import jax.numpy as jnp
from jax import lax
from jax.experimental import pallas as pl
from jax.experimental.pallas import tpu as pltpu
from jax.sharding import PartitionSpec as P

MESH = pl.DeviceIdType.MESH
PHASES = 4
RELAYED = 3
decay_rate = 0.95


def place():
    row, col = lax.axis_index("row"), lax.axis_index("col")
    return row // 8, lax.rem(row // 2, 4), lax.rem(row, 2), col // 2, lax.rem(col, 2)


def device(y, x, zh, zl, core):
    return ((y * 4 + x) * 2 + zh, zl * 2 + core)


def tiles(size, step):
    return [(start, min(step, size - start)) for start in range(0, size, step)]


def kernel(
    factor_hbm, root_hbm, grad_hbm, fresh, pre_ref,
    grad_ref, slots, own_in, cols, own, root, factor, part, pieces, core_in, sums, line_in, relay_in,
    load_sem, twin_sem, near_send, near_recv, far_send, far_recv, own_send, own_recv, across_sem, core_sem, line_send, line_recv, relay_sem,
):
    y, x, zh, zl, core = place()
    rows, depth = root.shape
    share = grad_hbm.shape[0]
    span = slots.shape[-1]
    block = 8 * share

    load_root = pltpu.make_async_copy(root_hbm, root, load_sem.at[0])
    load_factor = pltpu.make_async_copy(factor_hbm, factor, load_sem.at[1])
    load_grad = pltpu.make_async_copy(grad_hbm, grad_ref, load_sem.at[2])
    load_grad.start()

    def turned(a, k):
        return lax.rem(a + k, 4)

    barrier = pltpu.get_barrier_semaphore()
    peers = [device(y, x, 1 - zh, zl, core), device(y, x, zh, zl, 1 - core)]
    for k in (1, 2, 3):
        peers += [device(y, turned(x, k), zh, zl, core), device(turned(y, k), x, zh, zl, core)]
    for step in (1, 2, 3, 5, 6, 7):
        level = lax.rem(zh * 4 + zl + step, 8)
        peers.append(device(y, x, level // 4, lax.rem(level, 4), core))
    for peer in peers:
        pl.semaphore_signal(barrier, inc=1, device_id=peer, device_id_type=MESH)
    load_grad.wait()
    load_root.start()
    load_factor.start()
    for p in range(PHASES):
        slots[p, zh, y, x] = grad_ref[:, p * span : (p + 1) * span]
    pl.semaphore_wait(barrier, len(peers))
    edge = jnp.logical_or(zl == 0, zl == 3)

    def twin(p, side):
        at = slots.at[p, side, y, x]
        return pltpu.make_async_remote_copy(
            src_ref=at, dst_ref=at, send_sem=twin_sem.at[0, p], recv_sem=twin_sem.at[1, p],
            device_id=device(y, x, 1 - zh, zl, core), device_id_type=MESH,
        )

    def x_first(own_side, p):
        return (own_side + p) % 2 == 1

    def near(own_side, p, k, arriving):
        side = zh if own_side else 1 - zh
        back = 4 - k if arriving else 0
        if x_first(own_side, p):
            at = slots.at[p, side, y, turned(x, back)]
            target = device(y, turned(x, k), zh, zl, core)
        else:
            at = slots.at[p, side, turned(y, back), x]
            target = device(turned(y, k), x, zh, zl, core)
        s = (own_side * PHASES + p) * 3 + k - 1
        return pltpu.make_async_remote_copy(
            src_ref=at, dst_ref=at, send_sem=near_send.at[s], recv_sem=near_recv.at[s],
            device_id=target, device_id_type=MESH,
        )

    def far(own_side, p, k, half, origin, lane):
        side = zh if own_side else 1 - zh
        part_of = pl.ds(half * 2, 2)
        if x_first(own_side, p):
            at = slots.at[p, side, turned(y, origin), part_of]
            target = device(turned(y, k), x, zh, zl, core)
        else:
            at = slots.at[p, side, part_of, turned(x, origin)]
            target = device(y, turned(x, k), zh, zl, core)
        s = ((own_side * PHASES + p) * 3 + lane) * 2 + half
        return pltpu.make_async_remote_copy(
            src_ref=at, dst_ref=at, send_sem=far_send.at[s], recv_sem=far_recv.at[s],
            device_id=target, device_id_type=MESH,
        )

    def near_start(own_side, p):
        for k in (2, 1, 3):
            near(own_side, p, k, False).start()

    def far_start(own_side, p):
        for k in (1, 3, 2):
            near(own_side, p, k, True).wait_recv()
        for step in range(2):
            far(own_side, p, 1, step, 0, 0).start()
            far(own_side, p, 3, 1 - step, 0, 1).start()

    def far_pass(own_side, p):
        far(own_side, p, 1, 0, 3, 0).wait_recv()
        far(own_side, p, 1, 0, 3, 2).start()
        far(own_side, p, 3, 1, 1, 1).wait_recv()
        far(own_side, p, 3, 1, 1, 2).start()

    def far_wait(own_side, p):
        far(own_side, p, 1, 1, 3, 0).wait_recv()
        far(own_side, p, 3, 0, 1, 1).wait_recv()
        far(own_side, p, 1, 0, 2, 2).wait_recv()
        far(own_side, p, 3, 1, 2, 2).wait_recv()

    def gather_sent(p):
        for own_side in range(2):
            for k in (1, 2, 3):
                near(own_side, p, k, False).wait_send()
            for half in range(2):
                far(own_side, p, 1, half, 0, 0).wait_send()
                far(own_side, p, 3, half, 0, 1).wait_send()
            far(own_side, p, 1, 0, 3, 2).wait_send()
            far(own_side, p, 3, 1, 1, 2).wait_send()

    def twin_near(p):
        twin(p, 1 - zh).wait_recv()
        near_start(0, p)

    is_source = core == x // 2
    at_root = zl == y
    is_root = jnp.logical_and(is_source, at_root)
    is_end = jnp.logical_and(is_source, jnp.logical_not(at_root))

    def own_block(side):
        return lax.rem(x, 2) * 2 + side

    def own_far(p, n):
        step = (1, 7, 2, 6, 3, 5)[n]
        level = lax.rem(zh * 4 + zl + step, 8)
        return pltpu.make_async_remote_copy(
            src_ref=slots.at[p, zh, own_block(level // 4)], dst_ref=own_in.at[p, zh],
            send_sem=own_send.at[p, n], recv_sem=own_recv.at[p, zh],
            device_id=device(y, x, level // 4, lax.rem(level, 4), core), device_id_type=MESH,
        )

    def own_landed(p, side):
        at = own_in.at[p, side]
        return pltpu.make_async_remote_copy(
            src_ref=at, dst_ref=at, send_sem=own_send.at[p, 0], recv_sem=own_recv.at[p, side],
            device_id=device(y, x, zh, zl, 1 - core), device_id_type=MESH,
        )

    def own_across(p, from_root):
        lanes = pl.ds(p * span, span)
        here = own.at[:, lanes]
        src = here
        if from_root:
            src = cols.at[pl.ds(pl.multiple_of(own_block(zh) * block, 16), block), lanes]
        return pltpu.make_async_remote_copy(
            src_ref=src, dst_ref=here, send_sem=across_sem.at[0, p], recv_sem=across_sem.at[1, p],
            device_id=device(y, x, zh, zl, 1 - core), device_id_type=MESH,
        )

    def own_start(p):
        far_wait(1, p)

        @pl.when(is_root)
        def _():
            for n in range(6):
                own_far(p, n).start()

    def own_pass(p):
        @pl.when(is_root)
        def _():
            own_across(p, True).start()

        @pl.when(is_end)
        def _():
            own_landed(p, 0).wait_recv()
            own_landed(p, 1).wait_recv()
            parts = [own_in[p, s % 2, s // 2] for s in range(8)]
            own[:, pl.ds(p * span, span)] = jnp.concatenate(parts, 0)
            own_across(p, False).start()

    def own_wait(p):
        @pl.when(jnp.logical_not(is_source))
        def _():
            own_across(p, False).wait_recv()

    def own_sent(p):
        @pl.when(is_root)
        def _():
            for n in range(6):
                own_far(p, n).wait_send()

        @pl.when(is_source)
        def _():
            own_across(p, False).wait_send()

    def assemble(p):
        lanes = pl.ds(p * span, span)

        @pl.loop(0, 4)
        def _(yy):
            parts = [slots[p, s % 2, yy, s // 2] for s in range(8)]
            cols[pl.ds(pl.multiple_of(yy * block, 16), block), lanes] = jnp.concatenate(parts, 0)

    def multiply(p):
        lanes = pl.ds(p * span, span)

        def some(at, size):
            part[pl.ds(at, size), :] = jnp.dot(
                root[pl.ds(at, size), :], cols[:, lanes], preferred_element_type=jnp.float32
            )

        half = rows // 32 * 16
        some(0, half)
        some(half, rows - half)
        for s in range(8):
            pieces[p, s % 2, s // 2] = part[s * share : (s + 1) * share, :]

    def core_copy(p):
        return pltpu.make_async_remote_copy(
            src_ref=pieces.at[p, 1 - core], dst_ref=core_in.at[p],
            send_sem=core_sem.at[0, p], recv_sem=core_sem.at[1, p],
            device_id=device(y, x, zh, zl, 1 - core), device_id_type=MESH,
        )

    def line_copy(p, k):
        return pltpu.make_async_remote_copy(
            src_ref=sums.at[p, turned(zl, k)], dst_ref=line_in.at[p, k - 1],
            send_sem=line_send.at[p, k - 1], recv_sem=line_recv.at[p, k - 1],
            device_id=device(y, x, zh, turned(zl, k), core), device_id_type=MESH,
        )

    inner = jnp.logical_not(edge)
    inward = jnp.where(zl == 0, 1, 3)

    def relay_copy(p):
        return pltpu.make_async_remote_copy(
            src_ref=sums.at[p, 3 - zl], dst_ref=relay_in.at[p],
            send_sem=relay_sem.at[0, p], recv_sem=relay_sem.at[1, p],
            device_id=device(y, x, zh, turned(zl, inward), core), device_id_type=MESH,
        )

    def relayed(p):
        return p < RELAYED

    def reduce_start(p):
        core_copy(p).wait_recv()
        for s in range(4):
            sums[p, s] = pieces[p, core, s] + core_in[p, s]

        if not relayed(p):
            for k in (2, 1, 3):
                line_copy(p, k).start()
            return

        @pl.when(edge)
        def _():
            relay_copy(p).start()
            line_copy(p, 2).start()
            line_copy(p, inward).start()

        @pl.when(inner)
        def _():
            line_copy(p, 1).start()
            line_copy(p, 3).start()

    def reduce_relay(p):
        if not relayed(p):
            return

        @pl.when(inner)
        def _():
            relay_copy(p).wait_recv()
            sums[p, turned(zl, 2)] += relay_in[p]
            line_copy(p, 2).start()

    def reduce_end(p):
        line_copy(p, 2).wait_recv()

        @pl.when(jnp.logical_or(zl > 0, not relayed(p)))
        def _():
            line_copy(p, 1).wait_recv()
            sums[p, zl] += line_in[p, 0]

        @pl.when(jnp.logical_or(zl < 3, not relayed(p)))
        def _():
            line_copy(p, 3).wait_recv()
            sums[p, zl] += line_in[p, 2]

        total = sums[p, zl] + line_in[p, 1]
        pre_ref[:, p * span : (p + 1) * span] = total.astype(pre_ref.dtype)

    def reduce_sent(p):
        line_copy(p, 2).wait_send()

        @pl.when(jnp.logical_and(edge, relayed(p)))
        def _():
            relay_copy(p).wait_send()

        @pl.when(jnp.logical_or(zl < 3, not relayed(p)))
        def _():
            line_copy(p, 1).wait_send()

        @pl.when(jnp.logical_or(zl > 0, not relayed(p)))
        def _():
            line_copy(p, 3).wait_send()

    def finish(p):
        far_wait(0, p)
        assemble(p)
        multiply(p)
        core_copy(p).start()

    twin(0, zh).start()
    near_start(1, 0)
    twin(1, zh).start()
    near_start(1, 1)
    twin(2, zh).start()
    near_start(1, 2)
    twin(3, zh).start()
    near_start(1, 3)
    far_start(1, 0)
    far_start(1, 1)
    far_start(1, 2)
    far_start(1, 3)
    twin_near(0)
    twin_near(1)
    twin_near(2)
    twin_near(3)
    far_pass(1, 0)
    far_pass(1, 1)
    far_start(0, 0)
    own_start(0)
    far_pass(1, 2)
    far_start(0, 1)
    own_start(1)
    far_pass(1, 3)
    far_start(0, 2)
    own_start(2)
    far_pass(0, 0)
    far_start(0, 3)
    own_start(3)
    far_pass(0, 1)
    far_pass(0, 2)

    load_root.wait()
    finish(0)
    far_pass(0, 3)
    reduce_start(0)
    finish(1)
    reduce_start(1)
    finish(2)
    reduce_relay(0)
    reduce_start(2)
    finish(3)
    reduce_relay(1)
    reduce_start(3)
    own_pass(0)
    own_pass(1)
    reduce_relay(2)
    own_pass(2)
    own_pass(3)
    reduce_relay(3)

    for p in range(PHASES):
        own_wait(p)

    @pl.when(is_root)
    def _():
        own[...] = cols[pl.ds(pl.multiple_of(own_block(zh) * block, 16), block), :]

    load_factor.wait()

    def update(at, size):
        lanes = pl.ds(at, size)
        statistic = lax.dot_general(
            own[...], cols[lanes, :], (((1,), (1,)), ((), ())), preferred_element_type=jnp.float32
        )
        mixed = decay_rate * factor[:, lanes].astype(jnp.float32) + (1.0 - decay_rate) * statistic
        fresh[:, lanes] = mixed.astype(fresh.dtype)

    steps = tiles(depth, 256)

    @pl.loop(0, depth // 256)
    def _(i):
        update(pl.multiple_of(i * 256, 256), 256)

    if depth % 256:
        update(*steps[-1])
    for p in range(PHASES):
        reduce_end(p)
    for p in range(PHASES):
        twin(p, zh).wait_send()
        gather_sent(p)
        own_sent(p)
        core_copy(p).wait_send()
        reduce_sent(p)


def per_device(factor, inverse_root, gradients):
    rows, depth = factor.shape
    share, width = gradients.shape
    span = width // PHASES
    bf16, f32 = jnp.bfloat16, jnp.float32
    dma = pltpu.SemaphoreType.DMA
    flops = 4 * rows * depth * width
    return pl.pallas_call(
        kernel,
        out_shape=(
            pltpu.VMEM(factor.shape, bf16),
            pltpu.VMEM((share, width), bf16),
        ),
        in_specs=[
            pl.BlockSpec(memory_space=pltpu.HBM),
            pl.BlockSpec(memory_space=pltpu.HBM),
            pl.BlockSpec(memory_space=pltpu.HBM),
        ],
        out_specs=(pl.BlockSpec(memory_space=pltpu.VMEM), pl.BlockSpec(memory_space=pltpu.VMEM)),
        scratch_shapes=[
            pltpu.VMEM((share, width), bf16),
            pltpu.VMEM((PHASES, 2, 4, 4, share, span), bf16),
            pltpu.VMEM((PHASES, 2, 4, share, span), bf16),
            pltpu.VMEM((depth, width), bf16),
            pltpu.VMEM((rows, width), bf16),
            pltpu.VMEM((rows, depth), bf16),
            pltpu.VMEM((rows, depth), bf16),
            pltpu.VMEM((rows, span), f32),
            pltpu.VMEM((PHASES, 2, 4, share, span), f32),
            pltpu.VMEM((PHASES, 4, share, span), f32),
            pltpu.VMEM((PHASES, 4, share, span), f32),
            pltpu.VMEM((PHASES, 3, share, span), f32),
            pltpu.VMEM((PHASES, share, span), f32),
            dma((3,)),
            dma((2, PHASES)),
            dma((6 * PHASES,)),
            dma((6 * PHASES,)),
            dma((12 * PHASES,)),
            dma((12 * PHASES,)),
            dma((PHASES, 6)),
            dma((PHASES, 2)),
            dma((2, PHASES)),
            dma((2, PHASES)),
            dma((PHASES, 3)),
            dma((PHASES, 3)),
            dma((2, PHASES)),
        ],
        compiler_params=pltpu.CompilerParams(
            collective_id=0, has_side_effects=True, vmem_limit_bytes=48 * 1024 * 1024
        ),
        cost_estimate=pl.CostEstimate(flops=flops, bytes_accessed=6 * rows * depth, transcendentals=0),
    )(factor, inverse_root, gradients)


def solution(mesh):
    placed = (P("row", "col"), P("row", "col"), P(("col", "row"), None))
    return jax.shard_map(
        per_device,
        mesh=mesh,
        in_specs=placed,
        out_specs=(P("row", "col"), P(("row", "col"), None)),
        check_vma=False,
    )
```

```python
import functools

import jax
import jax.numpy as jnp
from jax import lax
from jax.experimental import pallas as pl
from jax.experimental.pallas import tpu as pltpu
from jax.sharding import PartitionSpec as P

MESH = pl.DeviceIdType.MESH
PHASES = 4
RELAYED = 3
FORWARDED = 2
decay_rate = 0.95


def place():
    row, col = lax.axis_index("row"), lax.axis_index("col")
    return row // 8, lax.rem(row // 2, 4), lax.rem(row, 2), col // 2, lax.rem(col, 2)


def device(y, x, zh, zl, core):
    return ((y * 4 + x) * 2 + zh, zl * 2 + core)


def tiles(size, step):
    return [(start, min(step, size - start)) for start in range(0, size, step)]


def kernel(
    factor_hbm, root_hbm, grad_hbm, fresh, pre_ref,
    grad_ref, slots, own_in, cols, own, root, factor, part, pieces, core_in, sums, line_in, relay_in,
    load_sem, twin_sem, near_send, near_recv, far_send, far_recv, own_send, own_recv, across_sem, core_sem, line_send, line_recv, relay_sem,
):
    y, x, zh, zl, core = place()
    rows, depth = root.shape
    share = grad_hbm.shape[0]
    span = slots.shape[-1]
    block = 8 * share

    load_root = pltpu.make_async_copy(root_hbm, root, load_sem.at[0])
    load_factor = pltpu.make_async_copy(factor_hbm, factor, load_sem.at[1])
    load_grad = pltpu.make_async_copy(grad_hbm, grad_ref, load_sem.at[2])
    load_grad.start()

    def turned(a, k):
        return lax.rem(a + k, 4)

    barrier = pltpu.get_barrier_semaphore()
    peers = [device(y, x, 1 - zh, zl, core), device(y, x, zh, zl, 1 - core)]
    for k in (1, 2, 3):
        peers += [device(y, turned(x, k), zh, zl, core), device(turned(y, k), x, zh, zl, core)]
    for step in (1, 2, 3, 5, 6, 7):
        level = lax.rem(zh * 4 + zl + step, 8)
        peers.append(device(y, x, level // 4, lax.rem(level, 4), core))
    for peer in peers:
        pl.semaphore_signal(barrier, inc=1, device_id=peer, device_id_type=MESH)
    load_grad.wait()
    load_root.start()
    load_factor.start()
    for p in range(PHASES):
        slots[p, zh, y, x] = grad_ref[:, p * span : (p + 1) * span]
    pl.semaphore_wait(barrier, len(peers))
    edge = jnp.logical_or(zl == 0, zl == 3)

    def twin(p, side):
        at = slots.at[p, side, y, x]
        return pltpu.make_async_remote_copy(
            src_ref=at, dst_ref=at, send_sem=twin_sem.at[0, p], recv_sem=twin_sem.at[1, p],
            device_id=device(y, x, 1 - zh, zl, core), device_id_type=MESH,
        )

    def x_first(own_side, p):
        return (own_side + p) % 2 == 1

    def near(own_side, p, k, arriving):
        side = zh if own_side else 1 - zh
        back = 4 - k if arriving else 0
        if x_first(own_side, p):
            at = slots.at[p, side, y, turned(x, back)]
            target = device(y, turned(x, k), zh, zl, core)
        else:
            at = slots.at[p, side, turned(y, back), x]
            target = device(turned(y, k), x, zh, zl, core)
        s = (own_side * PHASES + p) * 3 + k - 1
        return pltpu.make_async_remote_copy(
            src_ref=at, dst_ref=at, send_sem=near_send.at[s], recv_sem=near_recv.at[s],
            device_id=target, device_id_type=MESH,
        )

    def far(own_side, p, k, half, origin, lane):
        side = zh if own_side else 1 - zh
        part_of = pl.ds(half * 2, 2)
        if x_first(own_side, p):
            at = slots.at[p, side, turned(y, origin), part_of]
            target = device(turned(y, k), x, zh, zl, core)
        else:
            at = slots.at[p, side, part_of, turned(x, origin)]
            target = device(y, turned(x, k), zh, zl, core)
        s = ((own_side * PHASES + p) * 3 + lane) * 2 + half
        return pltpu.make_async_remote_copy(
            src_ref=at, dst_ref=at, send_sem=far_send.at[s], recv_sem=far_recv.at[s],
            device_id=target, device_id_type=MESH,
        )

    def near_start(own_side, p):
        for k in (2, 1, 3):
            near(own_side, p, k, False).start()

    def straight(own_side, p):
        return own_side == 0 and p >= FORWARDED

    def far_start(own_side, p):
        for k in (1, 3, 2):
            near(own_side, p, k, True).wait_recv()
        for step in range(2):
            far(own_side, p, 1, step, 0, 0).start()
            far(own_side, p, 3, 1 - step, 0, 1).start()
        if straight(own_side, p):
            for half in range(2):
                far(own_side, p, 2, half, 0, 2).start()

    def far_pass(own_side, p):
        far(own_side, p, 1, 0, 3, 0).wait_recv()
        if not straight(own_side, p):
            far(own_side, p, 1, 0, 3, 2).start()
        far(own_side, p, 3, 1, 1, 1).wait_recv()
        if not straight(own_side, p):
            far(own_side, p, 3, 1, 1, 2).start()

    def far_wait(own_side, p):
        far(own_side, p, 1, 1, 3, 0).wait_recv()
        far(own_side, p, 3, 0, 1, 1).wait_recv()
        far(own_side, p, 1, 0, 2, 2).wait_recv()
        far(own_side, p, 3, 1, 2, 2).wait_recv()

    def gather_sent(p):
        for own_side in range(2):
            for k in (1, 2, 3):
                near(own_side, p, k, False).wait_send()
            for half in range(2):
                far(own_side, p, 1, half, 0, 0).wait_send()
                far(own_side, p, 3, half, 0, 1).wait_send()
            far(own_side, p, 1, 0, 3, 2).wait_send()
            far(own_side, p, 3, 1, 1, 2).wait_send()

    def twin_near(p):
        twin(p, 1 - zh).wait_recv()
        near_start(0, p)

    is_source = core == x // 2
    at_root = zl == y
    is_root = jnp.logical_and(is_source, at_root)
    is_end = jnp.logical_and(is_source, jnp.logical_not(at_root))

    def own_block(side):
        return lax.rem(x, 2) * 2 + side

    def own_far(p, n):
        step = (1, 7, 2, 6, 3, 5)[n]
        level = lax.rem(zh * 4 + zl + step, 8)
        return pltpu.make_async_remote_copy(
            src_ref=slots.at[p, zh, own_block(level // 4)], dst_ref=own_in.at[p, zh],
            send_sem=own_send.at[p, n], recv_sem=own_recv.at[p, zh],
            device_id=device(y, x, level // 4, lax.rem(level, 4), core), device_id_type=MESH,
        )

    def own_landed(p, side):
        at = own_in.at[p, side]
        return pltpu.make_async_remote_copy(
            src_ref=at, dst_ref=at, send_sem=own_send.at[p, 0], recv_sem=own_recv.at[p, side],
            device_id=device(y, x, zh, zl, 1 - core), device_id_type=MESH,
        )

    def own_across(p, from_root):
        lanes = pl.ds(p * span, span)
        here = own.at[:, lanes]
        src = here
        if from_root:
            src = cols.at[pl.ds(pl.multiple_of(own_block(zh) * block, 16), block), lanes]
        return pltpu.make_async_remote_copy(
            src_ref=src, dst_ref=here, send_sem=across_sem.at[0, p], recv_sem=across_sem.at[1, p],
            device_id=device(y, x, zh, zl, 1 - core), device_id_type=MESH,
        )

    def own_start(p):
        far_wait(1, p)

        @pl.when(is_root)
        def _():
            for n in range(6):
                own_far(p, n).start()

    def own_pass(p):
        @pl.when(is_root)
        def _():
            own_across(p, True).start()

        @pl.when(is_end)
        def _():
            own_landed(p, 0).wait_recv()
            own_landed(p, 1).wait_recv()
            parts = [own_in[p, s % 2, s // 2] for s in range(8)]
            own[:, pl.ds(p * span, span)] = jnp.concatenate(parts, 0)
            own_across(p, False).start()

    def own_wait(p):
        @pl.when(jnp.logical_not(is_source))
        def _():
            own_across(p, False).wait_recv()

    def own_sent(p):
        @pl.when(is_root)
        def _():
            for n in range(6):
                own_far(p, n).wait_send()

        @pl.when(is_source)
        def _():
            own_across(p, False).wait_send()

    def assemble(p):
        lanes = pl.ds(p * span, span)

        @pl.loop(0, 4)
        def _(yy):
            parts = [slots[p, s % 2, yy, s // 2] for s in range(8)]
            cols[pl.ds(pl.multiple_of(yy * block, 16), block), lanes] = jnp.concatenate(parts, 0)

    def multiply(p):
        lanes = pl.ds(p * span, span)

        def some(at, size):
            part[pl.ds(at, size), :] = jnp.dot(
                root[pl.ds(at, size), :], cols[:, lanes], preferred_element_type=jnp.float32
            )

        half = rows // 32 * 16
        some(0, half)
        some(half, rows - half)
        for s in range(8):
            pieces[p, s % 2, s // 2] = part[s * share : (s + 1) * share, :]

    def core_copy(p):
        return pltpu.make_async_remote_copy(
            src_ref=pieces.at[p, 1 - core], dst_ref=core_in.at[p],
            send_sem=core_sem.at[0, p], recv_sem=core_sem.at[1, p],
            device_id=device(y, x, zh, zl, 1 - core), device_id_type=MESH,
        )

    def line_copy(p, k):
        return pltpu.make_async_remote_copy(
            src_ref=sums.at[p, turned(zl, k)], dst_ref=line_in.at[p, k - 1],
            send_sem=line_send.at[p, k - 1], recv_sem=line_recv.at[p, k - 1],
            device_id=device(y, x, zh, turned(zl, k), core), device_id_type=MESH,
        )

    inner = jnp.logical_not(edge)
    inward = jnp.where(zl == 0, 1, 3)

    def relay_copy(p):
        return pltpu.make_async_remote_copy(
            src_ref=sums.at[p, 3 - zl], dst_ref=relay_in.at[p],
            send_sem=relay_sem.at[0, p], recv_sem=relay_sem.at[1, p],
            device_id=device(y, x, zh, turned(zl, inward), core), device_id_type=MESH,
        )

    def relayed(p):
        return p < RELAYED

    def reduce_start(p):
        core_copy(p).wait_recv()
        for s in range(4):
            sums[p, s] = pieces[p, core, s] + core_in[p, s]

        if not relayed(p):
            for k in (2, 1, 3):
                line_copy(p, k).start()
            return

        @pl.when(edge)
        def _():
            relay_copy(p).start()
            line_copy(p, 2).start()
            line_copy(p, inward).start()

        @pl.when(inner)
        def _():
            line_copy(p, 1).start()
            line_copy(p, 3).start()

    def reduce_relay(p):
        if not relayed(p):
            return

        @pl.when(inner)
        def _():
            relay_copy(p).wait_recv()
            sums[p, turned(zl, 2)] += relay_in[p]
            line_copy(p, 2).start()

    def reduce_end(p):
        line_copy(p, 2).wait_recv()

        @pl.when(jnp.logical_or(zl > 0, not relayed(p)))
        def _():
            line_copy(p, 1).wait_recv()
            sums[p, zl] += line_in[p, 0]

        @pl.when(jnp.logical_or(zl < 3, not relayed(p)))
        def _():
            line_copy(p, 3).wait_recv()
            sums[p, zl] += line_in[p, 2]

        total = sums[p, zl] + line_in[p, 1]
        pre_ref[:, p * span : (p + 1) * span] = total.astype(pre_ref.dtype)

    def reduce_sent(p):
        line_copy(p, 2).wait_send()

        @pl.when(jnp.logical_and(edge, relayed(p)))
        def _():
            relay_copy(p).wait_send()

        @pl.when(jnp.logical_or(zl < 3, not relayed(p)))
        def _():
            line_copy(p, 1).wait_send()

        @pl.when(jnp.logical_or(zl > 0, not relayed(p)))
        def _():
            line_copy(p, 3).wait_send()

    def finish(p):
        far_wait(0, p)
        assemble(p)
        multiply(p)
        core_copy(p).start()

    twin(0, zh).start()
    near_start(1, 0)
    twin(1, zh).start()
    near_start(1, 1)
    twin(2, zh).start()
    near_start(1, 2)
    twin(3, zh).start()
    near_start(1, 3)
    far_start(1, 0)
    far_start(1, 1)
    far_start(1, 2)
    far_start(1, 3)
    twin_near(0)
    twin_near(1)
    twin_near(2)
    twin_near(3)
    far_pass(1, 0)
    far_pass(1, 1)
    far_start(0, 0)
    own_start(0)
    far_pass(1, 2)
    far_start(0, 1)
    own_start(1)
    far_pass(1, 3)
    far_start(0, 2)
    own_start(2)
    far_pass(0, 0)
    far_start(0, 3)
    own_start(3)
    far_pass(0, 1)
    far_pass(0, 2)

    load_root.wait()
    finish(0)
    far_pass(0, 3)
    reduce_start(0)
    finish(1)
    reduce_start(1)
    finish(2)
    reduce_relay(0)
    reduce_start(2)
    finish(3)
    reduce_relay(1)
    reduce_start(3)
    own_pass(0)
    own_pass(1)
    reduce_relay(2)
    own_pass(2)
    own_pass(3)
    reduce_relay(3)

    for p in range(PHASES):
        own_wait(p)

    @pl.when(is_root)
    def _():
        own[...] = cols[pl.ds(pl.multiple_of(own_block(zh) * block, 16), block), :]

    load_factor.wait()

    def update(at, size):
        lanes = pl.ds(at, size)
        statistic = lax.dot_general(
            own[...], cols[lanes, :], (((1,), (1,)), ((), ())), preferred_element_type=jnp.float32
        )
        mixed = decay_rate * factor[:, lanes].astype(jnp.float32) + (1.0 - decay_rate) * statistic
        fresh[:, lanes] = mixed.astype(fresh.dtype)

    steps = tiles(depth, 256)

    @pl.loop(0, depth // 256)
    def _(i):
        update(pl.multiple_of(i * 256, 256), 256)

    if depth % 256:
        update(*steps[-1])
    for p in range(PHASES):
        reduce_end(p)
    for p in range(PHASES):
        twin(p, zh).wait_send()
        gather_sent(p)
        own_sent(p)
        core_copy(p).wait_send()
        reduce_sent(p)


def per_device(factor, inverse_root, gradients):
    rows, depth = factor.shape
    share, width = gradients.shape
    span = width // PHASES
    bf16, f32 = jnp.bfloat16, jnp.float32
    dma = pltpu.SemaphoreType.DMA
    flops = 4 * rows * depth * width
    return pl.pallas_call(
        kernel,
        out_shape=(
            pltpu.VMEM(factor.shape, bf16),
            pltpu.VMEM((share, width), bf16),
        ),
        in_specs=[
            pl.BlockSpec(memory_space=pltpu.HBM),
            pl.BlockSpec(memory_space=pltpu.HBM),
            pl.BlockSpec(memory_space=pltpu.HBM),
        ],
        out_specs=(pl.BlockSpec(memory_space=pltpu.VMEM), pl.BlockSpec(memory_space=pltpu.VMEM)),
        scratch_shapes=[
            pltpu.VMEM((share, width), bf16),
            pltpu.VMEM((PHASES, 2, 4, 4, share, span), bf16),
            pltpu.VMEM((PHASES, 2, 4, share, span), bf16),
            pltpu.VMEM((depth, width), bf16),
            pltpu.VMEM((rows, width), bf16),
            pltpu.VMEM((rows, depth), bf16),
            pltpu.VMEM((rows, depth), bf16),
            pltpu.VMEM((rows, span), f32),
            pltpu.VMEM((PHASES, 2, 4, share, span), f32),
            pltpu.VMEM((PHASES, 4, share, span), f32),
            pltpu.VMEM((PHASES, 4, share, span), f32),
            pltpu.VMEM((PHASES, 3, share, span), f32),
            pltpu.VMEM((PHASES, share, span), f32),
            dma((3,)),
            dma((2, PHASES)),
            dma((6 * PHASES,)),
            dma((6 * PHASES,)),
            dma((12 * PHASES,)),
            dma((12 * PHASES,)),
            dma((PHASES, 6)),
            dma((PHASES, 2)),
            dma((2, PHASES)),
            dma((2, PHASES)),
            dma((PHASES, 3)),
            dma((PHASES, 3)),
            dma((2, PHASES)),
        ],
        compiler_params=pltpu.CompilerParams(
            collective_id=0, has_side_effects=True, vmem_limit_bytes=48 * 1024 * 1024
        ),
        cost_estimate=pl.CostEstimate(flops=flops, bytes_accessed=6 * rows * depth, transcendentals=0),
    )(factor, inverse_root, gradients)


def solution(mesh):
    placed = (P("row", "col"), P("row", "col"), P(("col", "row"), None))
    return jax.shard_map(
        per_device,
        mesh=mesh,
        in_specs=placed,
        out_specs=(P("row", "col"), P(("row", "col"), None)),
        check_vma=False,
    )
```
